32 devices in a mesh: fsdp: 2 (over x), ep: 16 (over z, y, core).
Axes of the slice: x: 2, y: 2, z: 4, core: 2. Of those that a mesh axis runs over, the one named last changes fastest.
Arguments:
- hidden_rows: bfloat16 [1024, 2, 4096], P('fsdp'), may hold values from -6 to 6
- norm_gain: float32 [4096], replicated, may hold values from 0.1 to 1.9
- route_expert: int32 [1024, 2, 2], P('fsdp'), may hold values from 0 to 3, all different within a row
- route_weight: float32 [1024, 2, 2], P('fsdp'), may hold values from 0.2 to 1
- gate_base: bfloat16 [16, 4096, 384], P('ep'), may hold values from -0.09375 to 0.09375
- up_base: bfloat16 [16, 4096, 384], P('ep'), may hold values from -0.09375 to 0.09375
- down_base: bfloat16 [16, 384, 4096], P('ep'), may hold values from -0.15625 to 0.15625
- tile_values: bfloat16 [1024, 128, 128], P(('fsdp', 'ep')), may hold values from -6 to 6
- tile_scale: float32 [1024], P(('fsdp', 'ep')), may hold values from 0.01 to 0.08
- tile_owner: int32 [1024, 1], P(('fsdp', 'ep')), may hold values from 0 to 15; in each aligned block of 32 rows (0 to 31, 32 to 63, ...) at most 4 rows name the same one
- tile_slot: int32 [1024], P(('fsdp', 'ep')), may hold values from 0 to 287
Outputs:
- layer_out: bfloat16 [1024, 2, 4096], P(('fsdp', 'ep'))
The draws below stay inside these ranges and needn't reach their ends.
Inputs may be any that keep to these rules, and one draw needn't show every extreme that they name: `tile_owner`: among the 32 tiles of one trainer device no owner is named more than 4 times. `route_expert`: each row and step names 2 different experts.
All inputs are finite; a program needn't handle non-finite values.
Results may differ from the reference program's by a relative error of at most 0.022.
Values may be sent and summed in bfloat16 or wider, within the bound.
A program may use at most 256 MiB of HBM per device.

```python
import math
import jax
import jax.numpy as jnp
import numpy as np
from jax import lax

D = 4096
FF = 1536
TB = 128
TSPLIT = 4
TOP = 2
STEPS = 2
TILE_DEV = 32
CAP = 4
HID = 384
EXPERTS = 4
TILES = 1024
SLOTS = 288
ROWS_ALL = 1024
N_EP = 16


def set_ends(result, rng, low, high):
    place = [jax.random.randint(jax.random.fold_in(rng, axis), (), 0, length) for axis, length in enumerate(result.shape)]
    longest = result.shape.index(max(result.shape))
    neighbour = place[:longest] + [(place[longest] + 1) % result.shape[longest]] + place[longest + 1:]
    return result.at[tuple(place)].set(low).at[tuple(neighbour)].set(high)


def levels(own_key, dims, shards, low, top_value):
    def one(dim, parts):
        heights = jax.random.uniform(jax.random.fold_in(jax.random.fold_in(own_key, 6), dim), (parts,), jnp.float32, low / len(shards), top_value / len(shards))
        return jnp.repeat(jnp.exp(heights), dims[dim] // parts).reshape((-1,) + (1,) * (len(dims) - dim - 1))

    level = one(*shards[0])
    for cut in shards[1:]:
        level = level * one(*cut)
    return level


def different_ones(stream_key, rows, number_of, top, lift):
    order = jax.random.permutation(jax.random.fold_in(stream_key, 1), number_of)
    favour = order
    for power in range(3):
        favour = favour * favour // number_of
    favour = favour * lift // number_of
    tickets = jax.random.randint(jax.random.fold_in(stream_key, 2), (rows, number_of), 0, 4096) + favour
    fixed_rows = jax.random.permutation(jax.random.fold_in(stream_key, 3), rows)[jnp.arange(number_of) % rows]
    tickets = jnp.where(jnp.arange(rows)[:, None] == fixed_rows[None, :], 1 << 14, tickets)
    score = tickets * number_of + jnp.arange(number_of)
    return lax.top_k(score.astype(jnp.int32), top)[1].astype(jnp.int32)


def shared_out(own_key, own, number, rows, number_of, top, limit, skew):
    sequence = jax.random.permutation(own_key, number_of)
    packed, common = shares(number_of, rows * top, limit, skew, True), shares(number_of, rows * top, limit, skew, False)
    places = jnp.arange(number_of)

    def named(tallies, rotation):
        used = int((tallies > 0).sum())
        fixed = max(1, used // 4)
        shifted = fixed + (places - fixed + rotation * (used - fixed)) % max(1, number_of - fixed)
        return jnp.zeros((number_of,), jnp.int32).at[sequence[jnp.where(places < fixed, places, shifted)]].set(jnp.asarray(tallies, jnp.int32))

    tallies = jnp.where(number % 4 == 0, named(packed, number // 4), named(common, number - number // 4 - 1))
    mixed = jax.random.permutation(jax.random.fold_in(own, 3), number_of)
    source_of, sink = mixed[0:number_of // 2 * 2:2], mixed[1:number_of // 2 * 2:2]
    margin = jnp.minimum(tallies[source_of] - 1, limit - tallies[sink]) // 2
    margin = jnp.where((source_of == sequence[0]) | (sink == sequence[0]) | (tallies[sink] == 0), 0, jnp.maximum(margin, 0))
    shifted = jax.random.randint(jax.random.fold_in(own, 4), (number_of // 2,), 0, 1 << 20) % (margin + 1)
    tallies = tallies.at[source_of].add(-shifted).at[sink].add(shifted)
    members = jnp.searchsorted(jnp.cumsum(tallies), jnp.arange(rows * top), side="right").astype(jnp.int32)
    grid = members.reshape(top, rows).T
    grid = grid[jax.random.permutation(jax.random.fold_in(own, 1), rows)]
    rotation = jax.random.randint(jax.random.fold_in(own, 2), (rows, 1), 0, top)
    return jnp.take_along_axis(grid, (jnp.arange(top)[None, :] + rotation) % top, axis=1)


def shares(count, total, reach, skew, full):
    loads = [(1 << 20) // math.isqrt(rank ** skew) + 1 for rank in range(1, count + 1)]
    largest = reach if full else min(reach, max(-(-total // count), total * loads[0] // sum(loads)))
    least = 1 if total - largest >= count - 1 else 0
    given, rest = [largest] + [least] * (count - 1), total - largest - least * (count - 1)
    while rest > 0:
        free = [i for i in range(1, count) if given[i] < largest] or [i for i in range(1, count) if given[i] < reach]
        pool, budget = sum([loads[i] for i in free]), rest
        for i in free:
            more = min(reach - given[i], max(1, budget * loads[i] // pool), rest)
            given[i] = given[i] + more
            rest = rest - more
    return np.array(given)


def bell_draw(key, dims, width, most, cuts=(), held_as=jnp.bfloat16):
    entries = width * jax.random.normal(key, dims, jnp.float32)
    if cuts:
        entries = entries * levels(key, dims, cuts, -0.22, 0.18)
    return jnp.clip(entries, -most, most).astype(held_as)


def setup_inputs(seed: int = 0) -> dict:
    key_list = jax.random.split(jax.random.key(seed), 12)
    hidden_rows = bell_draw(key_list[0], (ROWS_ALL, STEPS, D), 1.0, 6.0, ((0, 2),))
    norm_gain = jnp.clip(1.0 + 0.18 * jax.random.normal(key_list[1], (D,), jnp.float32), 0.1, 1.9)
    route_expert = different_ones(key_list[2], ROWS_ALL * STEPS, EXPERTS, TOP, 4096).reshape((ROWS_ALL, STEPS, TOP))
    route_weight = jnp.clip(0.2 + 0.8 * jax.random.uniform(key_list[3], (ROWS_ALL, STEPS, TOP), jnp.float32) ** levels(key_list[3], (ROWS_ALL, STEPS, TOP), ((0, 2),), -0.2, 0.2), 0.2, 1.0)
    gate_base = bell_draw(key_list[4], (N_EP, D, HID), D ** -0.5, 0.09375, ((0, 16),))
    up_base = bell_draw(key_list[5], (N_EP, D, HID), D ** -0.5, 0.09375, ((0, 16),))
    down_base = bell_draw(key_list[6], (N_EP, HID, D), FF ** -0.5, 0.15625, ((0, 16),))
    tile_values = bell_draw(key_list[7], (TILES, TB, TB), 1.0, 6.0, ((0, 32),))
    tile_scale = jnp.clip(jnp.exp(math.log(0.08) - 2.0794415 * jax.random.uniform(key_list[8], (TILES,), jnp.float32) ** levels(key_list[8], (TILES,), ((0, 32),), -0.2, 0.2)), 0.01, 0.08)
    tile_owner_keys = jax.random.split(jax.random.fold_in(key_list[9], 1), TILES // TILE_DEV)
    tile_owner_turns = jax.random.permutation(jax.random.fold_in(key_list[9], 3), TILES // TILE_DEV)
    tile_owner = jax.vmap(lambda own, number: shared_out(jax.random.fold_in(key_list[9], 2), own, number, TILE_DEV, N_EP, 1, CAP, 2))(tile_owner_keys, tile_owner_turns).reshape((TILES, 1))
    tile_slot = set_ends(jax.random.randint(key_list[10], (TILES,), 0, SLOTS), jax.random.fold_in(key_list[10], 1), 0, SLOTS - 1).astype(jnp.int32)
    return dict(hidden_rows=hidden_rows, norm_gain=norm_gain, route_expert=route_expert, route_weight=route_weight, gate_base=gate_base, up_base=up_base, down_base=down_base, tile_values=tile_values, tile_scale=tile_scale, tile_owner=tile_owner, tile_slot=tile_slot)


EPSILON = 1e-06

def normalize(hidden_rows, norm_gain):
    values = hidden_rows.astype(jnp.float32)
    scaled = values * lax.rsqrt(lax.optimization_barrier(jnp.mean(values * values, axis=-1, keepdims=True)) + EPSILON)
    return (scaled * norm_gain.astype(jnp.float32)).astype(jnp.bfloat16)

def unfold_delta(delta):
    row_blocks = D // TB
    col_blocks = HID // TB
    third = row_blocks * col_blocks
    gate_part = delta[:third].reshape(row_blocks, col_blocks, TB, TB).transpose(0, 2, 1, 3).reshape(D, HID)
    up_part = delta[third:2 * third].reshape(row_blocks, col_blocks, TB, TB).transpose(0, 2, 1, 3).reshape(D, HID)
    down_part = delta[2 * third:].reshape(col_blocks, row_blocks, TB, TB).transpose(0, 2, 1, 3).reshape(HID, D)
    return (gate_part, up_part, down_part)

def refreshed(gate_old, up_old, down_old, delta):
    gate_part, up_part, down_part = unfold_delta(delta)
    gate_new = (gate_old.astype(jnp.float32) + gate_part).astype(jnp.bfloat16)
    up_new = (up_old.astype(jnp.float32) + up_part).astype(jnp.bfloat16)
    down_new = (down_old.astype(jnp.float32) + down_part).astype(jnp.bfloat16)
    return (gate_new, up_new, down_new)

def expert_out(inputs, combine, gate_new, up_new, down_new):
    gate = jnp.dot(inputs, gate_new, preferred_element_type=jnp.float32)
    upward = jnp.dot(inputs, up_new, preferred_element_type=jnp.float32)
    hidden = (jax.nn.silu(gate) * upward * combine).astype(jnp.bfloat16)
    return jnp.dot(hidden, down_new, preferred_element_type=jnp.float32)

def reference(hidden_rows, norm_gain, route_expert, route_weight, gate_base, up_base, down_base, tile_values, tile_scale, tile_owner, tile_slot):
    owner_count = gate_base.shape[0]
    scaled_tiles = tile_values.astype(jnp.float32) * tile_scale[:, None, None]
    deltas = jnp.zeros((owner_count, SLOTS, TB, TB), jnp.float32).at[tile_owner[:, 0], tile_slot].add(scaled_tiles)
    normed = normalize(hidden_rows, norm_gain)
    inputs = normed.reshape(-1, D)

    def add_owner(total, owner):
        gate_new, up_new, down_new = refreshed(gate_base[owner], up_base[owner], down_base[owner], deltas[owner])
        expert = owner // TSPLIT
        combine = lax.optimization_barrier(jnp.sum(jnp.where(route_expert == expert, route_weight, 0.0), axis=-1)).reshape(-1, 1)
        return (total + expert_out(inputs, combine, gate_new, up_new, down_new), owner)
    total, unused = lax.scan(add_owner, jnp.zeros((inputs.shape[0], D), jnp.float32), jnp.arange(owner_count, dtype=jnp.int32))
    return total.reshape(hidden_rows.shape).astype(jnp.bfloat16)
```

```python
import functools

import jax
import jax.numpy as jnp
from jax import lax
from jax.experimental import pallas as pl
from jax.experimental.pallas import tpu as pltpu
from jax.sharding import PartitionSpec as P

MESH = pl.DeviceIdType.MESH
EPSILON = 1e-06
CAP = 4
LANES = 128


def xor(value, constant, size):
    result = 0
    bit = 1
    while bit < size:
        result = result + lax.rem(lax.div(value, bit) + (constant // bit) % 2, 2) * bit
        bit *= 2
    return result


def partner(me, step, size):
    return xor(me, step, size)


def pack_kernel(owner_ref, slot_ref, scale_ref, tiles_ref, out_ref, slots_ref, count_ref):
    held = tiles_ref.shape[0]
    owners, cap = out_ref.shape[:2]

    @pl.loop(0, owners)
    def _(o):
        count_ref[o] = 0
        for k in range(cap):
            slots_ref[o, 0, k] = -1

    @pl.loop(0, held)
    def _(t):
        o = owner_ref[t]
        k = count_ref[o]
        count_ref[o] = k + 1
        slots_ref[o, 0, k] = slot_ref[t]
        out_ref[o, k] = (tiles_ref[t].astype(jnp.float32) * scale_ref[t]).astype(out_ref.dtype)


def pack(tiles, scale, owner, slot, owners):
    edge = tiles.shape[1]
    smem = pl.BlockSpec(memory_space=pltpu.SMEM)
    vmem = pl.BlockSpec(memory_space=pltpu.VMEM)
    return pl.pallas_call(
        pack_kernel,
        out_shape=(
            jax.ShapeDtypeStruct((owners, CAP, edge, edge), jnp.bfloat16),
            jax.ShapeDtypeStruct((owners, 1, LANES), jnp.int32),
        ),
        in_specs=[smem, smem, smem, vmem],
        out_specs=(vmem, smem),
        scratch_shapes=[pltpu.SMEM((owners,), jnp.int32)],
        compiler_params=pltpu.CompilerParams(vmem_limit_bytes=24 << 20),
        name="pack",
    )(owner, slot, scale, tiles)


def exchange_kernel(
    n,
    groups,
    tiles_ref,
    slots_ref,
    rows_ref,
    gain_ref,
    tiles_out,
    slots_out,
    normed_out,
    row_in,
    row_out,
    in_sem,
    out_sem,
    own_sem,
    tile_send,
    tile_recv,
    slot_send,
    slot_recv,
    fwd_send,
    fwd_recv,
    fslot_send,
    fslot_recv,
):
    f = lax.axis_index("fsdp")
    e = lax.axis_index("ep")
    far = n // 2
    near_steps = list(range(1, far))
    far_steps = list(range(far, n))
    steps = []
    while near_steps or far_steps:
        if far_steps:
            steps.append(far_steps.pop(0))
        if near_steps:
            steps.append(near_steps.pop(0))

    barrier = pltpu.get_barrier_semaphore()
    for k in steps:
        pl.semaphore_signal(
            barrier, inc=1, device_id=(f, partner(e, k, n)), device_id_type=MESH
        )
    for g in range(1, groups):
        pl.semaphore_signal(
            barrier, inc=1, device_id=(lax.rem(f + g, groups), e), device_id_type=MESH
        )
    chunk = row_in.shape[1]
    chunks = rows_ref.shape[0] // chunk

    def load(i):
        return pltpu.make_async_copy(
            rows_ref.at[pl.ds(i * chunk, chunk)], row_in.at[i % 2], in_sem.at[i % 2]
        )

    def store(i):
        steps_dim = rows_ref.shape[1]
        return pltpu.make_async_copy(
            row_out.at[i % 2],
            normed_out.at[pl.ds(i * chunk * steps_dim, chunk * steps_dim)],
            out_sem.at[i % 2],
        )

    load(0).start()
    pl.semaphore_wait(barrier, n - 1 + groups - 1)

    waits = []

    def remote(src, dst, send, recv, target):
        copy = pltpu.make_async_remote_copy(
            src_ref=src,
            dst_ref=dst,
            send_sem=send,
            recv_sem=recv,
            device_id=target,
            device_id_type=MESH,
        )
        copy.start()
        waits.append(copy)
        return copy

    def forward(tile_src, slot_src, k, source):
        copies = []
        for g in range(1, groups):
            target = (lax.rem(f + g, groups), e)
            copies.append(
                remote(slot_src, slots_out.at[f, source], fslot_send.at[g, k],
                       fslot_recv.at[g, k], target)
            )
            copies.append(
                remote(tile_src, tiles_out.at[f, source], fwd_send.at[g, k],
                       fwd_recv.at[g, k], target)
            )
        return copies

    arrivals = {}
    forwards = forward(tiles_ref.at[e], slots_ref.at[e], 0, e)
    for k in steps:
        to = partner(e, k, n)
        slot_copy = remote(slots_ref.at[to], slots_out.at[f, e], slot_send.at[k],
                           slot_recv.at[k], (f, to))
        tile_copy = remote(tiles_ref.at[to], tiles_out.at[f, e], tile_send.at[k],
                           tile_recv.at[k], (f, to))
        arrivals[k] = (slot_copy, tile_copy)
    own = (
        pltpu.make_async_copy(tiles_ref.at[e], tiles_out.at[f, e], own_sem.at[0]),
        pltpu.make_async_copy(slots_ref.at[e], slots_out.at[f, e], own_sem.at[1]),
    )
    for copy in own:
        copy.start()

    def normalise(i):
        if i + 1 < chunks:
            load(i + 1).start()
        load(i).wait()
        if i >= 2:
            store(i - 2).wait()
        group = 8

        @pl.loop(0, chunk // group)
        def _(j):
            block = row_in[i % 2, pl.ds(j * group, group)].astype(jnp.float32)
            values = block.reshape(group * block.shape[1], block.shape[2])
            scaled = values * lax.rsqrt(
                jnp.mean(values * values, axis=-1, keepdims=True) + EPSILON
            )
            first = pl.multiple_of(j * values.shape[0], values.shape[0])
            row_out[i % 2, pl.ds(first, values.shape[0])] = (scaled * gain_ref[...]).astype(
                row_out.dtype
            )

        store(i).start()

    for i in range(max(chunks, len(steps))):
        if i < chunks:
            normalise(i)
        if i < len(steps):
            k = steps[i]
            source = partner(e, k, n)
            slot_copy, tile_copy = arrivals[k]
            slot_copy.wait_recv()
            tile_copy.wait_recv()
            forwards += forward(
                tiles_out.at[f, source], slots_out.at[f, source], k, source
            )
    for i in range(max(0, chunks - 2), chunks):
        store(i).wait()
    for copy in own:
        copy.wait()
    for copy in forwards:
        copy.wait_recv()
    for copy in waits:
        copy.wait_send()


def exchange(send_tiles, send_slots, hidden_rows, gain, groups):
    n, cap, edge, _ = send_tiles.shape
    rows, steps, width = hidden_rows.shape
    chunk = rows // 16
    any_spec = pl.BlockSpec(memory_space=pl.ANY)
    dma = pltpu.SemaphoreType.DMA
    return pl.pallas_call(
        functools.partial(exchange_kernel, n, groups),
        out_shape=(
            jax.ShapeDtypeStruct((groups, n, cap, edge, edge), jnp.bfloat16),
            jax.ShapeDtypeStruct((groups, n, 1, LANES), jnp.int32),
            jax.ShapeDtypeStruct((rows * steps, width), jnp.bfloat16),
        ),
        in_specs=[any_spec, any_spec, any_spec, pl.BlockSpec(memory_space=pltpu.VMEM)],
        out_specs=(any_spec, any_spec, any_spec),
        scratch_shapes=[
            pltpu.VMEM((2, chunk, steps, width), jnp.bfloat16),
            pltpu.VMEM((2, chunk * steps, width), jnp.bfloat16),
            dma((2,)),
            dma((2,)),
            dma((2,)),
            dma((n,)),
            dma((n,)),
            dma((n,)),
            dma((n,)),
            dma((groups, n)),
            dma((groups, n)),
            dma((groups, n)),
            dma((groups, n)),
        ],
        compiler_params=pltpu.CompilerParams(
            collective_id=0, has_side_effects=True, vmem_limit_bytes=24 << 20
        ),
        name="exchange",
    )(send_tiles, send_slots, hidden_rows, gain.reshape(1, -1))


def expert_kernel(
    slots_ref,
    tiles_ref,
    normed_ref,
    combine_ref,
    gate_ref,
    up_ref,
    down_ref,
    hidden_ref,
    down_new,
    tiles,
    normed,
    weights,
    total,
    head,
    chain,
    sems,
):
    hid = gate_ref.shape[2]
    width = gate_ref.shape[1]
    edge = tiles.shape[1]
    col_blocks = hid // edge
    row_blocks = width // edge
    third = row_blocks * col_blocks
    sources = slots_ref.shape[0]
    copies = [
        pltpu.make_async_copy(tiles_ref, tiles, sems.at[0]),
        pltpu.make_async_copy(gate_ref.at[0], weights.at[:, pl.ds(0, hid)], sems.at[1]),
        pltpu.make_async_copy(up_ref.at[0], weights.at[:, pl.ds(hid, hid)], sems.at[2]),
        pltpu.make_async_copy(down_ref.at[0], down_new, sems.at[3]),
        pltpu.make_async_copy(normed_ref, normed, sems.at[4]),
    ]
    for copy in copies:
        copy.start()

    @pl.loop(0, 3 * third)
    def _(s):
        head[s] = -1

    @pl.loop(0, sources)
    def _(d):
        for k in range(CAP):
            s = slots_ref[d, 0, k]

            @pl.when(s >= 0)
            def _():
                chain[d * CAP + k] = head[s]
                head[s] = d * CAP + k

    for copy in copies[:4]:
        copy.wait()

    def apply(s, target, rows, cols):
        first = head[s]

        @pl.when(first >= 0)
        def _():
            total[...] = target[rows, cols].astype(jnp.float32) + tiles[first].astype(jnp.float32)

            def more(entry):
                total[...] += tiles[entry].astype(jnp.float32)
                return chain[entry]

            lax.while_loop(lambda entry: entry >= 0, more, chain[first])
            target[rows, cols] = total[...].astype(target.dtype)

    @pl.loop(0, row_blocks)
    def _(r):
        span = pl.ds(pl.multiple_of(r * edge, edge), edge)
        for c in range(col_blocks):
            apply(r * col_blocks + c, weights, span, pl.ds(c * edge, edge))
            apply(third + r * col_blocks + c, weights, span, pl.ds(hid + c * edge, edge))
            apply(2 * third + c * row_blocks + r, down_new, pl.ds(c * edge, edge), span)

    copies[4].wait()
    block = 256

    @pl.loop(0, normed.shape[0] // block)
    def _(m):
        rows = pl.ds(pl.multiple_of(m * block, block), block)
        both = jnp.dot(normed[rows, :], weights[...], preferred_element_type=jnp.float32)
        gate = both[:, :hid]
        hidden_ref[rows, :] = (jax.nn.silu(gate) * both[:, hid:] * combine_ref[rows, :]).astype(
            hidden_ref.dtype
        )


def expert_hidden(slots, tiles, normed, combine, gate_base, up_base, down_base):
    rows, width = normed.shape
    hid = gate_base.shape[2]
    slot_count = 3 * gate_base.shape[1] * hid // (tiles.shape[1] ** 2)
    any_spec = pl.BlockSpec(memory_space=pl.ANY)
    vmem = pl.BlockSpec(memory_space=pltpu.VMEM)
    return pl.pallas_call(
        expert_kernel,
        out_shape=(
            jax.ShapeDtypeStruct((rows, hid), jnp.bfloat16),
            jax.ShapeDtypeStruct((hid, width), jnp.bfloat16),
        ),
        in_specs=[
            pl.BlockSpec(memory_space=pltpu.SMEM),
            any_spec,
            any_spec,
            vmem,
            any_spec,
            any_spec,
            any_spec,
        ],
        out_specs=(vmem, vmem),
        scratch_shapes=[
            pltpu.VMEM(tiles.shape, jnp.bfloat16),
            pltpu.VMEM((rows, width), jnp.bfloat16),
            pltpu.VMEM((width, 2 * hid), jnp.bfloat16),
            pltpu.VMEM(tiles.shape[1:], jnp.float32),
            pltpu.SMEM((slot_count,), jnp.int32),
            pltpu.SMEM((tiles.shape[0],), jnp.int32),
            pltpu.SemaphoreType.DMA((5,)),
        ],
        compiler_params=pltpu.CompilerParams(vmem_limit_bytes=52 << 20),
        name="expert",
    )(slots, tiles, normed, combine, gate_base, up_base, down_base)


def reduce_kernel(
    planes,
    parts,
    hidden_ref,
    down_ref,
    out_ref,
    part,
    core_buf,
    side_buf,
    line_buf,
    last_buf,
    core_send,
    core_recv,
    side_send,
    side_recv,
    line_send,
    line_recv,
    last_recv,
):
    f = lax.axis_index("fsdp")
    e = lax.axis_index("ep")
    z, y, c = lax.div(e, 4), lax.rem(lax.div(e, 2), 2), lax.rem(e, 2)
    core_peer = (f, z * 4 + y * 2 + (1 - c))
    side_peer = (f, z * 4 + (1 - y) * 2 + c)
    above = (f, lax.rem(e + 4, planes * 4))
    below = (f, lax.rem(e + planes * 4 - 4, planes * 4))
    chunk = part.shape[3]
    width = down_ref.shape[1]
    wide = width // parts
    tile = min(512, wide)

    barrier = pltpu.get_barrier_semaphore()
    pl.semaphore_signal(barrier, inc=1, device_id=core_peer, device_id_type=MESH)
    pl.semaphore_signal(barrier, inc=1, device_id=side_peer, device_id_type=MESH)

    @pl.when(z < planes - 1)
    def _():
        pl.semaphore_signal(barrier, inc=1, device_id=above, device_id_type=MESH)

    @pl.when(z > 0)
    def _():
        pl.semaphore_signal(barrier, inc=1, device_id=below, device_id_type=MESH)

    neighbours = jnp.where(z > 0, 1, 0) + jnp.where(z < planes - 1, 1, 0)
    pl.semaphore_wait(barrier, 2 + neighbours)

    table = [
        sorted(range(planes), key=lambda p, v=v: (-abs(p - v), -p if v < planes / 2 else p))
        for v in range(planes)
    ]

    def plane_of(step):
        return sum(jnp.where(z == v, table[v][step], 0) for v in range(planes))

    def remote(src, dst, send, recv, target):
        return pltpu.make_async_remote_copy(
            src_ref=src,
            dst_ref=dst,
            send_sem=send,
            recv_sem=recv,
            device_id=target,
            device_id_type=MESH,
        )

    pieces = [(step, h) for step in range(planes) for h in range(parts)]

    def core_copy(p, b):
        step, h = pieces[p]
        zz = plane_of(step)
        cols = pl.ds(h * wide, wide)
        return remote(
            part.at[zz, b, 1 - c, :, cols],
            core_buf.at[zz, b, :, cols],
            core_send.at[zz, h, b],
            core_recv.at[zz, h, b],
            core_peer,
        )

    def side_copy(p):
        step, h = pieces[p]
        zz = plane_of(step)
        cols = pl.ds(h * wide, wide)
        return remote(
            part.at[zz, 1 - y, c, :, cols],
            side_buf.at[zz, :, cols],
            side_send.at[zz, h],
            side_recv.at[zz, h],
            side_peer,
        )

    def line_copy(zz, h, target):
        cols = pl.ds(h * wide, wide)
        return remote(
            part.at[zz, y, c, :, cols],
            line_buf.at[zz, :, cols],
            line_send.at[zz, h],
            line_recv.at[zz, h],
            target,
        )

    def last_copy(zz, h, target):
        cols = pl.ds(h * wide, wide)
        return remote(
            part.at[zz, y, c, :, cols],
            last_buf.at[:, cols],
            line_send.at[zz, h],
            last_recv.at[h],
            target,
        )

    def compute(p):
        step, h = pieces[p]
        zz = plane_of(step)
        rows = pl.ds(pl.multiple_of(zz * 4 * chunk, 4 * chunk), 4 * chunk)

        @pl.loop(0, wide // tile)
        def _(j):
            cols = pl.ds(pl.multiple_of(h * wide + j * tile, tile), tile)
            product = jnp.dot(
                hidden_ref[rows, :], down_ref[:, cols], preferred_element_type=jnp.float32
            ).astype(part.dtype)
            part[zz, :, :, :, cols] = product.reshape(2, 2, chunk, tile)

        for b in range(2):
            core_copy(p, b).start()

    def pair(p):
        step, h = pieces[p]
        zz = plane_of(step)
        cols = pl.ds(h * wide, wide)
        for b in range(2):
            core_copy(p, b).wait_recv()
        for b in (1 - y, y):
            part[zz, b, c, :, cols] = (
                part[zz, b, c, :, cols].astype(jnp.float32)
                + core_buf[zz, b, :, cols].astype(jnp.float32)
            ).astype(part.dtype)
            if b is not y:
                side_copy(p).start()

    def line(p):
        step, h = pieces[p]
        zz = plane_of(step)
        cols = pl.ds(h * wide, wide)
        side_copy(p).wait_recv()

        def own():
            return part[zz, y, c, :, cols].astype(jnp.float32) + side_buf[zz, :, cols].astype(
                jnp.float32
            )

        if step < planes - 1:
            inner = ((zz > z) & (z > 0)) | ((zz < z) & (z < planes - 1))

            @pl.when(inner)
            def _():
                line_copy(zz, h, above).wait_recv()
                part[zz, y, c, :, cols] = (
                    own() + line_buf[zz, :, cols].astype(jnp.float32)
                ).astype(part.dtype)

            @pl.when(jnp.logical_not(inner))
            def _():
                part[zz, y, c, :, cols] = own().astype(part.dtype)

            @pl.when(zz > z)
            def _():
                line_copy(zz, h, above).start()

            @pl.when(zz == z - 1)
            def _():
                last_copy(zz, h, below).start()

            @pl.when(zz < z - 1)
            def _():
                line_copy(zz, h, below).start()
        else:
            out_ref[:, cols] = own()

            @pl.when(z > 0)
            def _():
                line_copy(zz, h, above).wait_recv()
                out_ref[:, cols] += line_buf[zz, :, cols].astype(jnp.float32)

            @pl.when(z < planes - 1)
            def _():
                last_copy(zz, h, below).wait_recv()
                out_ref[:, cols] += last_buf[:, cols].astype(jnp.float32)

    lag = 2 * parts
    for p in range(len(pieces) + 1):
        if p < len(pieces):
            compute(p)
        if p >= 1:
            pair(p - 1)
        if p >= lag + 1:
            line(p - 1 - lag)
    for p in range(len(pieces) - lag, len(pieces)):
        line(p)

    for p, (step, h) in enumerate(pieces):
        for b in range(2):
            core_copy(p, b).wait_send()
        side_copy(p).wait_send()
        if step < planes - 1:
            line_copy(plane_of(step), h, above).wait_send()


def down_and_reduce(hidden, down_new, n):
    rows, hid = hidden.shape
    width = down_new.shape[1]
    planes = n // 4
    chunk = rows // n
    parts = 2
    vmem = pl.BlockSpec(memory_space=pltpu.VMEM)
    dma = pltpu.SemaphoreType.DMA
    buf = lambda *shape: pltpu.VMEM(shape, jnp.bfloat16)
    return pl.pallas_call(
        functools.partial(reduce_kernel, planes, parts),
        out_shape=jax.ShapeDtypeStruct((chunk, width), jnp.float32),
        in_specs=[vmem, vmem],
        out_specs=vmem,
        scratch_shapes=[
            buf(planes, 2, 2, chunk, width),
            buf(planes, 2, chunk, width),
            buf(planes, chunk, width),
            buf(planes, chunk, width),
            buf(chunk, width),
            dma((planes, parts, 2)),
            dma((planes, parts, 2)),
            dma((planes, parts)),
            dma((planes, parts)),
            dma((planes, parts)),
            dma((planes, parts)),
            dma((parts,)),
        ],
        compiler_params=pltpu.CompilerParams(
            collective_id=1, has_side_effects=True, vmem_limit_bytes=44 << 20
        ),
        name="reduce",
    )(hidden, down_new)


def body(
    tsplit,
    hidden_rows,
    norm_gain,
    route_expert,
    route_weight,
    gate_base,
    up_base,
    down_base,
    tile_values,
    tile_scale,
    tile_owner,
    tile_slot,
):
    n = lax.axis_size("ep")
    groups = lax.axis_size("fsdp")
    rows, steps, width = hidden_rows.shape
    edge = tile_values.shape[1]
    send_tiles, send_slots = pack(tile_values, tile_scale, tile_owner[:, 0], tile_slot, n)
    expert = lax.axis_index("ep") // tsplit
    combine = jnp.sum(jnp.where(route_expert == expert, route_weight, 0.0), axis=-1)
    tiles, slots, normed = exchange(send_tiles, send_slots, hidden_rows, norm_gain, groups)
    hidden, down_new = expert_hidden(
        slots.reshape(groups * n, 1, LANES),
        tiles.reshape(groups * n * CAP, edge, edge),
        normed,
        combine.reshape(-1, 1),
        gate_base,
        up_base,
        down_base,
    )
    out = down_and_reduce(hidden, down_new, n)
    return out.reshape(rows // n, steps, width).astype(jnp.bfloat16)


TSPLIT = 4


def solution(mesh):
    return jax.shard_map(
        functools.partial(body, TSPLIT),
        mesh=mesh,
        in_specs=(
            P("fsdp", None, None),
            P(),
            P("fsdp", None, None),
            P("fsdp", None, None),
            P("ep", None, None),
            P("ep", None, None),
            P("ep", None, None),
            P(("fsdp", "ep"), None, None),
            P(("fsdp", "ep")),
            P(("fsdp", "ep"), None),
            P(("fsdp", "ep")),
        ),
        out_specs=P(("fsdp", "ep"), None, None),
        check_vma=False,
    )
```

```python
import functools

import jax
import jax.numpy as jnp
from jax import lax
from jax.experimental import pallas as pl
from jax.experimental.pallas import tpu as pltpu
from jax.sharding import PartitionSpec as P

MESH = pl.DeviceIdType.MESH
EPSILON = 1e-06
CAP = 4
LANES = 128


def xor(value, constant, size):
    result = 0
    bit = 1
    while bit < size:
        result = result + lax.rem(lax.div(value, bit) + (constant // bit) % 2, 2) * bit
        bit *= 2
    return result


def partner(me, step, size):
    return xor(me, step, size)


def pack_kernel(owner_ref, slot_ref, scale_ref, tiles_ref, out_ref, slots_ref, count_ref):
    held = tiles_ref.shape[0]
    owners, cap = out_ref.shape[:2]

    @pl.loop(0, owners)
    def _(o):
        count_ref[o] = 0
        for k in range(cap):
            slots_ref[o, 0, k] = -1

    @pl.loop(0, held)
    def _(t):
        o = owner_ref[t]
        k = count_ref[o]
        count_ref[o] = k + 1
        slots_ref[o, 0, k] = slot_ref[t]
        out_ref[o, k] = (tiles_ref[t].astype(jnp.float32) * scale_ref[t]).astype(out_ref.dtype)


def pack(tiles, scale, owner, slot, owners):
    edge = tiles.shape[1]
    smem = pl.BlockSpec(memory_space=pltpu.SMEM)
    vmem = pl.BlockSpec(memory_space=pltpu.VMEM)
    return pl.pallas_call(
        pack_kernel,
        out_shape=(
            jax.ShapeDtypeStruct((owners, CAP, edge, edge), jnp.bfloat16),
            jax.ShapeDtypeStruct((owners, 1, LANES), jnp.int32),
        ),
        in_specs=[smem, smem, smem, vmem],
        out_specs=(vmem, smem),
        scratch_shapes=[pltpu.SMEM((owners,), jnp.int32)],
        compiler_params=pltpu.CompilerParams(vmem_limit_bytes=24 << 20),
        name="pack",
    )(owner, slot, scale, tiles)


def exchange_kernel(
    n,
    groups,
    tiles_ref,
    slots_ref,
    rows_ref,
    gain_ref,
    tiles_out,
    slots_out,
    normed_out,
    row_in,
    row_out,
    in_sem,
    out_sem,
    own_sem,
    tile_send,
    tile_recv,
    slot_send,
    slot_recv,
    fwd_send,
    fwd_recv,
    fslot_send,
    fslot_recv,
):
    f = lax.axis_index("fsdp")
    e = lax.axis_index("ep")
    steps = list(range(1, n))

    barrier = pltpu.get_barrier_semaphore()
    for k in steps:
        pl.semaphore_signal(
            barrier, inc=1, device_id=(f, partner(e, k, n)), device_id_type=MESH
        )
    for g in range(1, groups):
        pl.semaphore_signal(
            barrier, inc=1, device_id=(lax.rem(f + g, groups), e), device_id_type=MESH
        )
    chunk = row_in.shape[1]
    chunks = rows_ref.shape[0] // chunk

    def load(i):
        return pltpu.make_async_copy(
            rows_ref.at[pl.ds(i * chunk, chunk)], row_in.at[i % 2], in_sem.at[i % 2]
        )

    def store(i):
        steps_dim = rows_ref.shape[1]
        return pltpu.make_async_copy(
            row_out.at[i % 2],
            normed_out.at[pl.ds(i * chunk * steps_dim, chunk * steps_dim)],
            out_sem.at[i % 2],
        )

    load(0).start()
    pl.semaphore_wait(barrier, n - 1 + groups - 1)

    waits = []

    def remote(src, dst, send, recv, target):
        copy = pltpu.make_async_remote_copy(
            src_ref=src,
            dst_ref=dst,
            send_sem=send,
            recv_sem=recv,
            device_id=target,
            device_id_type=MESH,
        )
        copy.start()
        waits.append(copy)
        return copy

    def forward(tile_src, slot_src, k, source):
        copies = []
        for g in range(1, groups):
            target = (lax.rem(f + g, groups), e)
            copies.append(
                remote(slot_src, slots_out.at[f, source], fslot_send.at[g, k],
                       fslot_recv.at[g, k], target)
            )
            copies.append(
                remote(tile_src, tiles_out.at[f, source], fwd_send.at[g, k],
                       fwd_recv.at[g, k], target)
            )
        return copies

    arrivals = {}
    forwards = forward(tiles_ref.at[e], slots_ref.at[e], 0, e)
    for k in steps:
        to = partner(e, k, n)
        slot_copy = remote(slots_ref.at[to], slots_out.at[f, e], slot_send.at[k],
                           slot_recv.at[k], (f, to))
        tile_copy = remote(tiles_ref.at[to], tiles_out.at[f, e], tile_send.at[k],
                           tile_recv.at[k], (f, to))
        arrivals[k] = (slot_copy, tile_copy)
    own = (
        pltpu.make_async_copy(tiles_ref.at[e], tiles_out.at[f, e], own_sem.at[0]),
        pltpu.make_async_copy(slots_ref.at[e], slots_out.at[f, e], own_sem.at[1]),
    )
    for copy in own:
        copy.start()

    def normalise(i):
        if i + 1 < chunks:
            load(i + 1).start()
        load(i).wait()
        if i >= 2:
            store(i - 2).wait()
        group = 8

        @pl.loop(0, chunk // group)
        def _(j):
            block = row_in[i % 2, pl.ds(j * group, group)].astype(jnp.float32)
            values = block.reshape(group * block.shape[1], block.shape[2])
            scaled = values * lax.rsqrt(
                jnp.mean(values * values, axis=-1, keepdims=True) + EPSILON
            )
            first = pl.multiple_of(j * values.shape[0], values.shape[0])
            row_out[i % 2, pl.ds(first, values.shape[0])] = (scaled * gain_ref[...]).astype(
                row_out.dtype
            )

        store(i).start()

    for i in range(max(chunks, len(steps))):
        if i < chunks:
            normalise(i)
        if i < len(steps):
            k = steps[i]
            source = partner(e, k, n)
            slot_copy, tile_copy = arrivals[k]
            slot_copy.wait_recv()
            tile_copy.wait_recv()
            forwards += forward(
                tiles_out.at[f, source], slots_out.at[f, source], k, source
            )
    for i in range(max(0, chunks - 2), chunks):
        store(i).wait()
    for copy in own:
        copy.wait()
    for copy in forwards:
        copy.wait_recv()
    for copy in waits:
        copy.wait_send()


def exchange(send_tiles, send_slots, hidden_rows, gain, groups):
    n, cap, edge, _ = send_tiles.shape
    rows, steps, width = hidden_rows.shape
    chunk = rows // 16
    any_spec = pl.BlockSpec(memory_space=pl.ANY)
    dma = pltpu.SemaphoreType.DMA
    return pl.pallas_call(
        functools.partial(exchange_kernel, n, groups),
        out_shape=(
            jax.ShapeDtypeStruct((groups, n, cap, edge, edge), jnp.bfloat16),
            jax.ShapeDtypeStruct((groups, n, 1, LANES), jnp.int32),
            jax.ShapeDtypeStruct((rows * steps, width), jnp.bfloat16),
        ),
        in_specs=[any_spec, any_spec, any_spec, pl.BlockSpec(memory_space=pltpu.VMEM)],
        out_specs=(any_spec, any_spec, any_spec),
        scratch_shapes=[
            pltpu.VMEM((2, chunk, steps, width), jnp.bfloat16),
            pltpu.VMEM((2, chunk * steps, width), jnp.bfloat16),
            dma((2,)),
            dma((2,)),
            dma((2,)),
            dma((n,)),
            dma((n,)),
            dma((n,)),
            dma((n,)),
            dma((groups, n)),
            dma((groups, n)),
            dma((groups, n)),
            dma((groups, n)),
        ],
        compiler_params=pltpu.CompilerParams(
            collective_id=0, has_side_effects=True, vmem_limit_bytes=60 << 20
        ),
        name="exchange",
    )(send_tiles, send_slots, hidden_rows, gain.reshape(1, -1))


def expert_kernel(
    slots_ref,
    tiles_ref,
    normed_ref,
    combine_ref,
    gate_ref,
    up_ref,
    down_ref,
    hidden_ref,
    down_new,
    tiles,
    normed,
    weights,
    total,
    head,
    chain,
    sems,
):
    hid = gate_ref.shape[2]
    width = gate_ref.shape[1]
    edge = tiles.shape[1]
    col_blocks = hid // edge
    row_blocks = width // edge
    third = row_blocks * col_blocks
    sources = slots_ref.shape[0]
    copies = [
        pltpu.make_async_copy(tiles_ref, tiles, sems.at[0]),
        pltpu.make_async_copy(gate_ref.at[0], weights.at[:, pl.ds(0, hid)], sems.at[1]),
        pltpu.make_async_copy(up_ref.at[0], weights.at[:, pl.ds(hid, hid)], sems.at[2]),
        pltpu.make_async_copy(down_ref.at[0], down_new, sems.at[3]),
        pltpu.make_async_copy(normed_ref, normed, sems.at[4]),
    ]
    for copy in copies:
        copy.start()

    @pl.loop(0, 3 * third)
    def _(s):
        head[s] = -1

    @pl.loop(0, sources)
    def _(d):
        for k in range(CAP):
            s = slots_ref[d, 0, k]

            @pl.when(s >= 0)
            def _():
                chain[d * CAP + k] = head[s]
                head[s] = d * CAP + k

    for copy in copies[:4]:
        copy.wait()

    def apply(s, target, rows, cols):
        first = head[s]

        @pl.when(first >= 0)
        def _():
            total[...] = target[rows, cols].astype(jnp.float32) + tiles[first].astype(jnp.float32)

            def more(entry):
                total[...] += tiles[entry].astype(jnp.float32)
                return chain[entry]

            lax.while_loop(lambda entry: entry >= 0, more, chain[first])
            target[rows, cols] = total[...].astype(target.dtype)

    @pl.loop(0, row_blocks)
    def _(r):
        span = pl.ds(pl.multiple_of(r * edge, edge), edge)
        for c in range(col_blocks):
            apply(r * col_blocks + c, weights, span, pl.ds(c * edge, edge))
            apply(third + r * col_blocks + c, weights, span, pl.ds(hid + c * edge, edge))
            apply(2 * third + c * row_blocks + r, down_new, pl.ds(c * edge, edge), span)

    copies[4].wait()
    block = 256

    @pl.loop(0, normed.shape[0] // block)
    def _(m):
        rows = pl.ds(pl.multiple_of(m * block, block), block)
        both = jnp.dot(normed[rows, :], weights[...], preferred_element_type=jnp.float32)
        gate = both[:, :hid]
        hidden_ref[rows, :] = (jax.nn.silu(gate) * both[:, hid:] * combine_ref[rows, :]).astype(
            hidden_ref.dtype
        )


def expert_hidden(slots, tiles, normed, combine, gate_base, up_base, down_base):
    rows, width = normed.shape
    hid = gate_base.shape[2]
    slot_count = 3 * gate_base.shape[1] * hid // (tiles.shape[1] ** 2)
    any_spec = pl.BlockSpec(memory_space=pl.ANY)
    vmem = pl.BlockSpec(memory_space=pltpu.VMEM)
    return pl.pallas_call(
        expert_kernel,
        out_shape=(
            jax.ShapeDtypeStruct((rows, hid), jnp.bfloat16),
            jax.ShapeDtypeStruct((hid, width), jnp.bfloat16),
        ),
        in_specs=[
            pl.BlockSpec(memory_space=pltpu.SMEM),
            any_spec,
            any_spec,
            vmem,
            any_spec,
            any_spec,
            any_spec,
        ],
        out_specs=(vmem, vmem),
        scratch_shapes=[
            pltpu.VMEM(tiles.shape, jnp.bfloat16),
            pltpu.VMEM((rows, width), jnp.bfloat16),
            pltpu.VMEM((width, 2 * hid), jnp.bfloat16),
            pltpu.VMEM(tiles.shape[1:], jnp.float32),
            pltpu.SMEM((slot_count,), jnp.int32),
            pltpu.SMEM((tiles.shape[0],), jnp.int32),
            pltpu.SemaphoreType.DMA((5,)),
        ],
        compiler_params=pltpu.CompilerParams(vmem_limit_bytes=52 << 20),
        name="expert",
    )(slots, tiles, normed, combine, gate_base, up_base, down_base)


def reduce_kernel(
    planes,
    parts,
    hidden_ref,
    down_ref,
    out_ref,
    part,
    core_buf,
    side_buf,
    line_buf,
    last_buf,
    core_send,
    core_recv,
    side_send,
    side_recv,
    line_send,
    line_recv,
    last_recv,
):
    f = lax.axis_index("fsdp")
    e = lax.axis_index("ep")
    z, y, c = lax.div(e, 4), lax.rem(lax.div(e, 2), 2), lax.rem(e, 2)
    core_peer = (f, z * 4 + y * 2 + (1 - c))
    side_peer = (f, z * 4 + (1 - y) * 2 + c)
    above = (f, lax.rem(e + 4, planes * 4))
    below = (f, lax.rem(e + planes * 4 - 4, planes * 4))
    chunk = part.shape[3]
    width = down_ref.shape[1]
    wide = width // parts
    tile = min(512, wide)

    barrier = pltpu.get_barrier_semaphore()
    pl.semaphore_signal(barrier, inc=1, device_id=core_peer, device_id_type=MESH)
    pl.semaphore_signal(barrier, inc=1, device_id=side_peer, device_id_type=MESH)

    @pl.when(z < planes - 1)
    def _():
        pl.semaphore_signal(barrier, inc=1, device_id=above, device_id_type=MESH)

    @pl.when(z > 0)
    def _():
        pl.semaphore_signal(barrier, inc=1, device_id=below, device_id_type=MESH)

    neighbours = jnp.where(z > 0, 1, 0) + jnp.where(z < planes - 1, 1, 0)
    pl.semaphore_wait(barrier, 2 + neighbours)

    table = [
        sorted(range(planes), key=lambda p, v=v: (-abs(p - v), -p if v < planes / 2 else p))
        for v in range(planes)
    ]

    def plane_of(step):
        return sum(jnp.where(z == v, table[v][step], 0) for v in range(planes))

    def remote(src, dst, send, recv, target):
        return pltpu.make_async_remote_copy(
            src_ref=src,
            dst_ref=dst,
            send_sem=send,
            recv_sem=recv,
            device_id=target,
            device_id_type=MESH,
        )

    pieces = [(step, h) for step in range(planes) for h in range(parts)]

    def core_copy(p, b):
        step, h = pieces[p]
        zz = plane_of(step)
        cols = pl.ds(h * wide, wide)
        return remote(
            part.at[zz, b, 1 - c, :, cols],
            core_buf.at[zz, b, :, cols],
            core_send.at[zz, h, b],
            core_recv.at[zz, h, b],
            core_peer,
        )

    def side_copy(p):
        step, h = pieces[p]
        zz = plane_of(step)
        cols = pl.ds(h * wide, wide)
        return remote(
            part.at[zz, 1 - y, c, :, cols],
            side_buf.at[zz, :, cols],
            side_send.at[zz, h],
            side_recv.at[zz, h],
            side_peer,
        )

    def line_copy(zz, h, target):
        cols = pl.ds(h * wide, wide)
        return remote(
            part.at[zz, y, c, :, cols],
            line_buf.at[zz, :, cols],
            line_send.at[zz, h],
            line_recv.at[zz, h],
            target,
        )

    def last_copy(zz, h, target):
        cols = pl.ds(h * wide, wide)
        return remote(
            part.at[zz, y, c, :, cols],
            last_buf.at[:, cols],
            line_send.at[zz, h],
            last_recv.at[h],
            target,
        )

    def compute(p):
        step, h = pieces[p]
        zz = plane_of(step)
        rows = pl.ds(pl.multiple_of(zz * 4 * chunk, 4 * chunk), 4 * chunk)

        @pl.loop(0, wide // tile)
        def _(j):
            cols = pl.ds(pl.multiple_of(h * wide + j * tile, tile), tile)
            product = jnp.dot(
                hidden_ref[rows, :], down_ref[:, cols], preferred_element_type=jnp.float32
            ).astype(part.dtype)
            part[zz, :, :, :, cols] = product.reshape(2, 2, chunk, tile)

        for b in range(2):
            core_copy(p, b).start()

    def pair(p):
        step, h = pieces[p]
        zz = plane_of(step)
        cols = pl.ds(h * wide, wide)
        for b in range(2):
            core_copy(p, b).wait_recv()
        for b in (1 - y, y):
            part[zz, b, c, :, cols] = (
                part[zz, b, c, :, cols].astype(jnp.float32)
                + core_buf[zz, b, :, cols].astype(jnp.float32)
            ).astype(part.dtype)
            if b is not y:
                side_copy(p).start()

    def line(p):
        step, h = pieces[p]
        zz = plane_of(step)
        cols = pl.ds(h * wide, wide)
        side_copy(p).wait_recv()

        def own():
            return part[zz, y, c, :, cols].astype(jnp.float32) + side_buf[zz, :, cols].astype(
                jnp.float32
            )

        if step < planes - 1:
            inner = ((zz > z) & (z > 0)) | ((zz < z) & (z < planes - 1))

            @pl.when(inner)
            def _():
                line_copy(zz, h, above).wait_recv()
                part[zz, y, c, :, cols] = (
                    own() + line_buf[zz, :, cols].astype(jnp.float32)
                ).astype(part.dtype)

            @pl.when(jnp.logical_not(inner))
            def _():
                part[zz, y, c, :, cols] = own().astype(part.dtype)

            @pl.when(zz > z)
            def _():
                line_copy(zz, h, above).start()

            @pl.when(zz == z - 1)
            def _():
                last_copy(zz, h, below).start()

            @pl.when(zz < z - 1)
            def _():
                line_copy(zz, h, below).start()
        else:
            out_ref[:, cols] = own()

            @pl.when(z > 0)
            def _():
                line_copy(zz, h, above).wait_recv()
                out_ref[:, cols] += line_buf[zz, :, cols].astype(jnp.float32)

            @pl.when(z < planes - 1)
            def _():
                last_copy(zz, h, below).wait_recv()
                out_ref[:, cols] += last_buf[:, cols].astype(jnp.float32)

    lag = 2 * parts
    for p in range(len(pieces) + 1):
        if p < len(pieces):
            compute(p)
        if p >= 1:
            pair(p - 1)
        if p >= lag + 1:
            line(p - 1 - lag)
    for p in range(len(pieces) - lag, len(pieces)):
        line(p)

    for p, (step, h) in enumerate(pieces):
        for b in range(2):
            core_copy(p, b).wait_send()
        side_copy(p).wait_send()
        if step < planes - 1:
            line_copy(plane_of(step), h, above).wait_send()


def down_and_reduce(hidden, down_new, n):
    rows, hid = hidden.shape
    width = down_new.shape[1]
    planes = n // 4
    chunk = rows // n
    parts = 2
    vmem = pl.BlockSpec(memory_space=pltpu.VMEM)
    dma = pltpu.SemaphoreType.DMA
    buf = lambda *shape: pltpu.VMEM(shape, jnp.bfloat16)
    return pl.pallas_call(
        functools.partial(reduce_kernel, planes, parts),
        out_shape=jax.ShapeDtypeStruct((chunk, width), jnp.float32),
        in_specs=[vmem, vmem],
        out_specs=vmem,
        scratch_shapes=[
            buf(planes, 2, 2, chunk, width),
            buf(planes, 2, chunk, width),
            buf(planes, chunk, width),
            buf(planes, chunk, width),
            buf(chunk, width),
            dma((planes, parts, 2)),
            dma((planes, parts, 2)),
            dma((planes, parts)),
            dma((planes, parts)),
            dma((planes, parts)),
            dma((planes, parts)),
            dma((parts,)),
        ],
        compiler_params=pltpu.CompilerParams(
            collective_id=1, has_side_effects=True, vmem_limit_bytes=44 << 20
        ),
        name="reduce",
    )(hidden, down_new)


def body(
    tsplit,
    hidden_rows,
    norm_gain,
    route_expert,
    route_weight,
    gate_base,
    up_base,
    down_base,
    tile_values,
    tile_scale,
    tile_owner,
    tile_slot,
):
    n = lax.axis_size("ep")
    groups = lax.axis_size("fsdp")
    rows, steps, width = hidden_rows.shape
    edge = tile_values.shape[1]
    send_tiles, send_slots = pack(tile_values, tile_scale, tile_owner[:, 0], tile_slot, n)
    expert = lax.axis_index("ep") // tsplit
    combine = jnp.sum(jnp.where(route_expert == expert, route_weight, 0.0), axis=-1)
    tiles, slots, normed = exchange(send_tiles, send_slots, hidden_rows, norm_gain, groups)
    hidden, down_new = expert_hidden(
        slots.reshape(groups * n, 1, LANES),
        tiles.reshape(groups * n * CAP, edge, edge),
        normed,
        combine.reshape(-1, 1),
        gate_base,
        up_base,
        down_base,
    )
    out = down_and_reduce(hidden, down_new, n)
    return out.reshape(rows // n, steps, width).astype(jnp.bfloat16)


TSPLIT = 4


def solution(mesh):
    return jax.shard_map(
        functools.partial(body, TSPLIT),
        mesh=mesh,
        in_specs=(
            P("fsdp", None, None),
            P(),
            P("fsdp", None, None),
            P("fsdp", None, None),
            P("ep", None, None),
            P("ep", None, None),
            P("ep", None, None),
            P(("fsdp", "ep"), None, None),
            P(("fsdp", "ep")),
            P(("fsdp", "ep"), None),
            P(("fsdp", "ep")),
        ),
        out_specs=P(("fsdp", "ep"), None, None),
        check_vma=False,
    )
```

```python
import functools

import jax
import jax.numpy as jnp
from jax import lax
from jax.experimental import pallas as pl
from jax.experimental.pallas import tpu as pltpu
from jax.sharding import PartitionSpec as P

MESH = pl.DeviceIdType.MESH
EPSILON = 1e-06
CAP = 4
LANES = 128


def xor(value, constant, size):
    result = 0
    bit = 1
    while bit < size:
        result = result + lax.rem(lax.div(value, bit) + (constant // bit) % 2, 2) * bit
        bit *= 2
    return result


def partner(me, step, size):
    return xor(me, step, size)


def pack_kernel(owner_ref, slot_ref, scale_ref, tiles_ref, out_ref, slots_ref, count_ref):
    held = tiles_ref.shape[0]
    owners, cap = out_ref.shape[:2]

    @pl.loop(0, owners)
    def _(o):
        count_ref[o] = 0
        for k in range(cap):
            slots_ref[o, 0, k] = -1

    @pl.loop(0, held)
    def _(t):
        o = owner_ref[t]
        k = count_ref[o]
        count_ref[o] = k + 1
        slots_ref[o, 0, k] = slot_ref[t]
        out_ref[o, k] = (tiles_ref[t].astype(jnp.float32) * scale_ref[t]).astype(out_ref.dtype)


def pack(tiles, scale, owner, slot, owners):
    edge = tiles.shape[1]
    smem = pl.BlockSpec(memory_space=pltpu.SMEM)
    vmem = pl.BlockSpec(memory_space=pltpu.VMEM)
    return pl.pallas_call(
        pack_kernel,
        out_shape=(
            jax.ShapeDtypeStruct((owners, CAP, edge, edge), jnp.bfloat16),
            jax.ShapeDtypeStruct((owners, 1, LANES), jnp.int32),
        ),
        in_specs=[smem, smem, smem, vmem],
        out_specs=(vmem, smem),
        scratch_shapes=[pltpu.SMEM((owners,), jnp.int32)],
        compiler_params=pltpu.CompilerParams(vmem_limit_bytes=24 << 20),
        name="pack",
    )(owner, slot, scale, tiles)


def exchange_kernel(
    n,
    groups,
    tiles_ref,
    slots_ref,
    rows_ref,
    gain_ref,
    tiles_out,
    slots_out,
    normed_out,
    row_in,
    row_out,
    in_sem,
    out_sem,
    own_sem,
    tile_send,
    tile_recv,
    slot_send,
    slot_recv,
    fwd_send,
    fwd_recv,
    fslot_send,
    fslot_recv,
):
    f = lax.axis_index("fsdp")
    e = lax.axis_index("ep")
    steps = list(range(1, n))

    barrier = pltpu.get_barrier_semaphore()
    for k in steps:
        pl.semaphore_signal(
            barrier, inc=1, device_id=(f, partner(e, k, n)), device_id_type=MESH
        )
    for g in range(1, groups):
        pl.semaphore_signal(
            barrier, inc=1, device_id=(lax.rem(f + g, groups), e), device_id_type=MESH
        )
    chunk = row_in.shape[1]
    chunks = rows_ref.shape[0] // chunk

    def load(i):
        return pltpu.make_async_copy(
            rows_ref.at[pl.ds(i * chunk, chunk)], row_in.at[i % 2], in_sem.at[i % 2]
        )

    def store(i):
        steps_dim = rows_ref.shape[1]
        return pltpu.make_async_copy(
            row_out.at[i % 2],
            normed_out.at[pl.ds(i * chunk * steps_dim, chunk * steps_dim)],
            out_sem.at[i % 2],
        )

    load(0).start()
    pl.semaphore_wait(barrier, n - 1 + groups - 1)

    waits = []

    def remote(src, dst, send, recv, target):
        copy = pltpu.make_async_remote_copy(
            src_ref=src,
            dst_ref=dst,
            send_sem=send,
            recv_sem=recv,
            device_id=target,
            device_id_type=MESH,
        )
        copy.start()
        waits.append(copy)
        return copy

    def forward(tile_src, slot_src, k, source):
        copies = []
        for g in range(1, groups):
            target = (lax.rem(f + g, groups), e)
            copies.append(
                remote(slot_src, slots_out.at[f, source], fslot_send.at[g, k],
                       fslot_recv.at[g, k], target)
            )
            copies.append(
                remote(tile_src, tiles_out.at[f, source], fwd_send.at[g, k],
                       fwd_recv.at[g, k], target)
            )
        return copies

    arrivals = {}
    forwards = forward(tiles_ref.at[e], slots_ref.at[e], 0, e)
    for k in steps:
        to = partner(e, k, n)
        slot_copy = remote(slots_ref.at[to], slots_out.at[f, e], slot_send.at[k],
                           slot_recv.at[k], (f, to))
        tile_copy = remote(tiles_ref.at[to], tiles_out.at[f, e], tile_send.at[k],
                           tile_recv.at[k], (f, to))
        arrivals[k] = (slot_copy, tile_copy)
    own = (
        pltpu.make_async_copy(tiles_ref.at[e], tiles_out.at[f, e], own_sem.at[0]),
        pltpu.make_async_copy(slots_ref.at[e], slots_out.at[f, e], own_sem.at[1]),
    )
    for copy in own:
        copy.start()

    def normalise(i):
        if i + 1 < chunks:
            load(i + 1).start()
        load(i).wait()
        if i >= 2:
            store(i - 2).wait()
        group = 8

        @pl.loop(0, chunk // group)
        def _(j):
            block = row_in[i % 2, pl.ds(j * group, group)].astype(jnp.float32)
            values = block.reshape(group * block.shape[1], block.shape[2])
            scaled = values * lax.rsqrt(
                jnp.mean(values * values, axis=-1, keepdims=True) + EPSILON
            )
            first = pl.multiple_of(j * values.shape[0], values.shape[0])
            row_out[i % 2, pl.ds(first, values.shape[0])] = (scaled * gain_ref[...]).astype(
                row_out.dtype
            )

        store(i).start()

    for i in range(max(chunks, len(steps))):
        if i < chunks:
            normalise(i)
        if i < len(steps):
            k = steps[i]
            source = partner(e, k, n)
            slot_copy, tile_copy = arrivals[k]
            slot_copy.wait_recv()
            tile_copy.wait_recv()
            forwards += forward(
                tiles_out.at[f, source], slots_out.at[f, source], k, source
            )
    for i in range(max(0, chunks - 2), chunks):
        store(i).wait()
    for copy in own:
        copy.wait()
    for copy in forwards:
        copy.wait_recv()
    for copy in waits:
        copy.wait_send()


def exchange(send_tiles, send_slots, hidden_rows, gain, groups):
    n, cap, edge, _ = send_tiles.shape
    rows, steps, width = hidden_rows.shape
    chunk = rows // 16
    any_spec = pl.BlockSpec(memory_space=pl.ANY)
    dma = pltpu.SemaphoreType.DMA
    return pl.pallas_call(
        functools.partial(exchange_kernel, n, groups),
        out_shape=(
            jax.ShapeDtypeStruct((groups, n, cap, edge, edge), jnp.bfloat16),
            jax.ShapeDtypeStruct((groups, n, 1, LANES), jnp.int32),
            jax.ShapeDtypeStruct((rows * steps, width), jnp.bfloat16),
        ),
        in_specs=[any_spec, any_spec, any_spec, pl.BlockSpec(memory_space=pltpu.VMEM)],
        out_specs=(any_spec, any_spec, any_spec),
        scratch_shapes=[
            pltpu.VMEM((2, chunk, steps, width), jnp.bfloat16),
            pltpu.VMEM((2, chunk * steps, width), jnp.bfloat16),
            dma((2,)),
            dma((2,)),
            dma((2,)),
            dma((n,)),
            dma((n,)),
            dma((n,)),
            dma((n,)),
            dma((groups, n)),
            dma((groups, n)),
            dma((groups, n)),
            dma((groups, n)),
        ],
        compiler_params=pltpu.CompilerParams(
            collective_id=0, has_side_effects=True, vmem_limit_bytes=60 << 20
        ),
        name="exchange",
    )(send_tiles, send_slots, hidden_rows, gain.reshape(1, -1))


def expert_kernel(
    slots_ref,
    tiles_ref,
    normed_ref,
    combine_ref,
    gate_ref,
    up_ref,
    down_ref,
    hidden_ref,
    down_new,
    tiles,
    normed,
    weights,
    total,
    head,
    chain,
    sems,
):
    hid = gate_ref.shape[2]
    width = gate_ref.shape[1]
    edge = tiles.shape[1]
    col_blocks = hid // edge
    row_blocks = width // edge
    third = row_blocks * col_blocks
    sources = slots_ref.shape[0]
    copies = [
        pltpu.make_async_copy(tiles_ref, tiles, sems.at[0]),
        pltpu.make_async_copy(gate_ref.at[0], weights.at[:, pl.ds(0, hid)], sems.at[1]),
        pltpu.make_async_copy(up_ref.at[0], weights.at[:, pl.ds(hid, hid)], sems.at[2]),
        pltpu.make_async_copy(down_ref.at[0], down_new, sems.at[3]),
        pltpu.make_async_copy(normed_ref, normed, sems.at[4]),
    ]
    for copy in copies:
        copy.start()

    @pl.loop(0, 3 * third)
    def _(s):
        head[s] = -1

    @pl.loop(0, sources)
    def _(d):
        for k in range(CAP):
            s = slots_ref[d, 0, k]

            @pl.when(s >= 0)
            def _():
                chain[d * CAP + k] = head[s]
                head[s] = d * CAP + k

    for copy in copies[:4]:
        copy.wait()

    def apply(s, target, rows, cols):
        first = head[s]

        @pl.when(first >= 0)
        def _():
            total[...] = target[rows, cols].astype(jnp.float32) + tiles[first].astype(jnp.float32)

            def more(entry):
                total[...] += tiles[entry].astype(jnp.float32)
                return chain[entry]

            lax.while_loop(lambda entry: entry >= 0, more, chain[first])
            target[rows, cols] = total[...].astype(target.dtype)

    @pl.loop(0, row_blocks)
    def _(r):
        span = pl.ds(pl.multiple_of(r * edge, edge), edge)
        for c in range(col_blocks):
            apply(r * col_blocks + c, weights, span, pl.ds(c * edge, edge))
            apply(third + r * col_blocks + c, weights, span, pl.ds(hid + c * edge, edge))
            apply(2 * third + c * row_blocks + r, down_new, pl.ds(c * edge, edge), span)

    copies[4].wait()
    block = 256

    @pl.loop(0, normed.shape[0] // block)
    def _(m):
        rows = pl.ds(pl.multiple_of(m * block, block), block)
        both = jnp.dot(normed[rows, :], weights[...], preferred_element_type=jnp.float32)
        gate = both[:, :hid]
        hidden_ref[rows, :] = (jax.nn.silu(gate) * both[:, hid:] * combine_ref[rows, :]).astype(
            hidden_ref.dtype
        )


def expert_hidden(slots, tiles, normed, combine, gate_base, up_base, down_base):
    rows, width = normed.shape
    hid = gate_base.shape[2]
    slot_count = 3 * gate_base.shape[1] * hid // (tiles.shape[1] ** 2)
    any_spec = pl.BlockSpec(memory_space=pl.ANY)
    vmem = pl.BlockSpec(memory_space=pltpu.VMEM)
    return pl.pallas_call(
        expert_kernel,
        out_shape=(
            jax.ShapeDtypeStruct((rows, hid), jnp.bfloat16),
            jax.ShapeDtypeStruct((hid, width), jnp.bfloat16),
        ),
        in_specs=[
            pl.BlockSpec(memory_space=pltpu.SMEM),
            any_spec,
            any_spec,
            vmem,
            any_spec,
            any_spec,
            any_spec,
        ],
        out_specs=(vmem, vmem),
        scratch_shapes=[
            pltpu.VMEM(tiles.shape, jnp.bfloat16),
            pltpu.VMEM((rows, width), jnp.bfloat16),
            pltpu.VMEM((width, 2 * hid), jnp.bfloat16),
            pltpu.VMEM(tiles.shape[1:], jnp.float32),
            pltpu.SMEM((slot_count,), jnp.int32),
            pltpu.SMEM((tiles.shape[0],), jnp.int32),
            pltpu.SemaphoreType.DMA((5,)),
        ],
        compiler_params=pltpu.CompilerParams(vmem_limit_bytes=52 << 20),
        name="expert",
    )(slots, tiles, normed, combine, gate_base, up_base, down_base)


def reduce_kernel(
    planes,
    parts,
    hidden_ref,
    down_ref,
    out_ref,
    part,
    core_buf,
    side_buf,
    line_buf,
    last_buf,
    core_send,
    core_recv,
    side_send,
    side_recv,
    line_send,
    line_recv,
    last_recv,
):
    f = lax.axis_index("fsdp")
    e = lax.axis_index("ep")
    z, y, c = lax.div(e, 4), lax.rem(lax.div(e, 2), 2), lax.rem(e, 2)
    core_peer = (f, z * 4 + y * 2 + (1 - c))
    side_peer = (f, z * 4 + (1 - y) * 2 + c)
    above = (f, lax.rem(e + 4, planes * 4))
    below = (f, lax.rem(e + planes * 4 - 4, planes * 4))
    chunk = part.shape[3]
    width = down_ref.shape[1]
    wide = width // parts
    tile = min(512, wide)

    barrier = pltpu.get_barrier_semaphore()
    pl.semaphore_signal(barrier, inc=1, device_id=core_peer, device_id_type=MESH)
    pl.semaphore_signal(barrier, inc=1, device_id=side_peer, device_id_type=MESH)

    @pl.when(z < planes - 1)
    def _():
        pl.semaphore_signal(barrier, inc=1, device_id=above, device_id_type=MESH)

    @pl.when(z > 0)
    def _():
        pl.semaphore_signal(barrier, inc=1, device_id=below, device_id_type=MESH)

    neighbours = jnp.where(z > 0, 1, 0) + jnp.where(z < planes - 1, 1, 0)
    pl.semaphore_wait(barrier, 2 + neighbours)

    table = [
        sorted(range(planes), key=lambda p, v=v: (-abs(p - v), -p if v < planes / 2 else p))
        for v in range(planes)
    ]

    def plane_of(step):
        return sum(jnp.where(z == v, table[v][step], 0) for v in range(planes))

    def remote(src, dst, send, recv, target):
        return pltpu.make_async_remote_copy(
            src_ref=src,
            dst_ref=dst,
            send_sem=send,
            recv_sem=recv,
            device_id=target,
            device_id_type=MESH,
        )

    pieces = [(step, h) for step in range(planes) for h in range(parts)]

    def core_copy(p, b):
        step, h = pieces[p]
        zz = plane_of(step)
        cols = pl.ds(h * wide, wide)
        return remote(
            part.at[zz, b, 1 - c, :, cols],
            core_buf.at[zz, b, :, cols],
            core_send.at[zz, h, b],
            core_recv.at[zz, h, b],
            core_peer,
        )

    def side_copy(p):
        step, h = pieces[p]
        zz = plane_of(step)
        cols = pl.ds(h * wide, wide)
        return remote(
            part.at[zz, 1 - y, c, :, cols],
            side_buf.at[zz, :, cols],
            side_send.at[zz, h],
            side_recv.at[zz, h],
            side_peer,
        )

    def line_copy(zz, h, target):
        cols = pl.ds(h * wide, wide)
        return remote(
            part.at[zz, y, c, :, cols],
            line_buf.at[zz, :, cols],
            line_send.at[zz, h],
            line_recv.at[zz, h],
            target,
        )

    def last_copy(zz, h, target):
        cols = pl.ds(h * wide, wide)
        return remote(
            part.at[zz, y, c, :, cols],
            last_buf.at[:, cols],
            line_send.at[zz, h],
            last_recv.at[h],
            target,
        )

    def compute(p):
        step, h = pieces[p]
        zz = plane_of(step)
        rows = pl.ds(pl.multiple_of(zz * 4 * chunk, 4 * chunk), 4 * chunk)

        @pl.loop(0, wide // tile)
        def _(j):
            cols = pl.ds(pl.multiple_of(h * wide + j * tile, tile), tile)
            product = jnp.dot(
                hidden_ref[rows, :], down_ref[:, cols], preferred_element_type=jnp.float32
            ).astype(part.dtype)
            part[zz, :, :, :, cols] = product.reshape(2, 2, chunk, tile)

        for b in range(2):
            core_copy(p, b).start()

    def pair(p):
        step, h = pieces[p]
        zz = plane_of(step)
        cols = pl.ds(h * wide, wide)
        for b in range(2):
            core_copy(p, b).wait_recv()
        for b in (1 - y, y):
            part[zz, b, c, :, cols] = (
                part[zz, b, c, :, cols].astype(jnp.float32)
                + core_buf[zz, b, :, cols].astype(jnp.float32)
            ).astype(part.dtype)
            if b is not y:
                side_copy(p).start()

    def line(p):
        step, h = pieces[p]
        zz = plane_of(step)
        cols = pl.ds(h * wide, wide)
        side_copy(p).wait_recv()

        def own():
            return part[zz, y, c, :, cols].astype(jnp.float32) + side_buf[zz, :, cols].astype(
                jnp.float32
            )

        if step < planes - 1:
            inner = ((zz > z) & (z > 0)) | ((zz < z) & (z < planes - 1))

            @pl.when(inner)
            def _():
                line_copy(zz, h, above).wait_recv()
                part[zz, y, c, :, cols] = (
                    own() + line_buf[zz, :, cols].astype(jnp.float32)
                ).astype(part.dtype)

            @pl.when(jnp.logical_not(inner))
            def _():
                part[zz, y, c, :, cols] = own().astype(part.dtype)

            @pl.when(zz > z)
            def _():
                line_copy(zz, h, above).start()

            @pl.when(zz == z - 1)
            def _():
                last_copy(zz, h, below).start()

            @pl.when(zz < z - 1)
            def _():
                line_copy(zz, h, below).start()
        else:
            out_ref[:, cols] = own()

            @pl.when(z > 0)
            def _():
                line_copy(zz, h, above).wait_recv()
                out_ref[:, cols] += line_buf[zz, :, cols].astype(jnp.float32)

            @pl.when(z < planes - 1)
            def _():
                last_copy(zz, h, below).wait_recv()
                out_ref[:, cols] += last_buf[:, cols].astype(jnp.float32)

    lag = 2 * parts
    for p in range(len(pieces) + 1):
        if p < len(pieces):
            compute(p)
        if p >= 1:
            pair(p - 1)
        if p >= lag + 1:
            line(p - 1 - lag)
    for p in range(len(pieces) - lag, len(pieces)):
        line(p)

    for p, (step, h) in enumerate(pieces):
        for b in range(2):
            core_copy(p, b).wait_send()
        side_copy(p).wait_send()
        if step < planes - 1:
            line_copy(plane_of(step), h, above).wait_send()


def down_and_reduce(hidden, down_new, n):
    rows, hid = hidden.shape
    width = down_new.shape[1]
    planes = n // 4
    chunk = rows // n
    parts = 4
    vmem = pl.BlockSpec(memory_space=pltpu.VMEM)
    dma = pltpu.SemaphoreType.DMA
    buf = lambda *shape: pltpu.VMEM(shape, jnp.bfloat16)
    return pl.pallas_call(
        functools.partial(reduce_kernel, planes, parts),
        out_shape=jax.ShapeDtypeStruct((chunk, width), jnp.float32),
        in_specs=[vmem, vmem],
        out_specs=vmem,
        scratch_shapes=[
            buf(planes, 2, 2, chunk, width),
            buf(planes, 2, chunk, width),
            buf(planes, chunk, width),
            buf(planes, chunk, width),
            buf(chunk, width),
            dma((planes, parts, 2)),
            dma((planes, parts, 2)),
            dma((planes, parts)),
            dma((planes, parts)),
            dma((planes, parts)),
            dma((planes, parts)),
            dma((parts,)),
        ],
        compiler_params=pltpu.CompilerParams(
            collective_id=1, has_side_effects=True, vmem_limit_bytes=44 << 20
        ),
        name="reduce",
    )(hidden, down_new)


def body(
    tsplit,
    hidden_rows,
    norm_gain,
    route_expert,
    route_weight,
    gate_base,
    up_base,
    down_base,
    tile_values,
    tile_scale,
    tile_owner,
    tile_slot,
):
    n = lax.axis_size("ep")
    groups = lax.axis_size("fsdp")
    rows, steps, width = hidden_rows.shape
    edge = tile_values.shape[1]
    send_tiles, send_slots = pack(tile_values, tile_scale, tile_owner[:, 0], tile_slot, n)
    expert = lax.axis_index("ep") // tsplit
    combine = jnp.sum(jnp.where(route_expert == expert, route_weight, 0.0), axis=-1)
    tiles, slots, normed = exchange(send_tiles, send_slots, hidden_rows, norm_gain, groups)
    hidden, down_new = expert_hidden(
        slots.reshape(groups * n, 1, LANES),
        tiles.reshape(groups * n * CAP, edge, edge),
        normed,
        combine.reshape(-1, 1),
        gate_base,
        up_base,
        down_base,
    )
    out = down_and_reduce(hidden, down_new, n)
    return out.reshape(rows // n, steps, width).astype(jnp.bfloat16)


TSPLIT = 4


def solution(mesh):
    return jax.shard_map(
        functools.partial(body, TSPLIT),
        mesh=mesh,
        in_specs=(
            P("fsdp", None, None),
            P(),
            P("fsdp", None, None),
            P("fsdp", None, None),
            P("ep", None, None),
            P("ep", None, None),
            P("ep", None, None),
            P(("fsdp", "ep"), None, None),
            P(("fsdp", "ep")),
            P(("fsdp", "ep"), None),
            P(("fsdp", "ep")),
        ),
        out_specs=P(("fsdp", "ep"), None, None),
        check_vma=False,
    )
```
